32 devices in a mesh: grp: 8 (over z, core), brk: 4 (over y, x).
Axes of the slice: x: 2, y: 2, z: 4, core: 2. Of those that a mesh axis runs over, the one named last changes fastest.
Arguments:
- state: float32 [8, 5, 192, 64, 128], P('grp', None, 'brk'), may hold values from -6 to 6
- adjoint: float32 [8, 5, 192, 64, 128], P('grp', None, 'brk'), may hold values from -6 to 6
- source: float32 [8, 5, 192, 64, 128], P('grp', None, 'brk'), may hold values from -6 to 6
- kappa: float32 [8, 192, 64, 128], P('grp', 'brk'), may hold values from 0.2 to 3
- cut_flags: int32 [8, 192, 64, 128], P('grp', 'brk'), may hold values 0 or 1
- coupling: float32 [5, 5], replicated, may hold values from -2.5 to 2.5
- target: int32 [32, 128], replicated, may hold values from 0 to 4095, as said below
Outputs:
- estimate: float32 [4096, 5, 384], P(('grp', 'brk'))
The draws below stay inside these ranges and needn't reach their ends.
Inputs may be any that keep to these rules, and one draw needn't show every extreme that they name: `target`: each value owner * 128 + slot appears exactly once; the owner is never in the sender's own level group; a brick sends at most 5 tiles to one owner, and exactly 5 to some owners.
All inputs are finite; a program needn't handle non-finite values. No bound on the sum of `cut_flags` on one device may be relied on, other than what follows from the above.
Results may differ from the reference program's by a relative error of at most 0.00007.
Values sent between devices are 32-bit elements; how exact they have to be, the bound alone decides.
A program may use at most 512 MiB of HBM per device.

```python
import math
import jax
import jax.numpy as jnp
from jax import lax

FIELDS = 5
BY = 64
BZ = 128
TPD = 128
NGROUP = 8
NBRICK = 4
OWNERS = 32
NX = 192
TILE = 384


def draw_target(key, part):
    pair_count = (NGROUP - 1) * NBRICK
    owner_count = NGROUP * NBRICK
    key_pairs, key_tiles, key_slots = jax.random.split(key, 3)
    cycled = jnp.arange(TPD, dtype=jnp.int32) % pair_count
    relabel = jax.random.permutation(key_pairs, pair_count).astype(jnp.int32)
    shift_id = relabel[cycled]
    shift_grp = 1 + shift_id // NBRICK
    shift_brk = shift_id % NBRICK
    devices = jnp.arange(owner_count, dtype=jnp.int32)
    group_of = devices // NBRICK
    brick_of = devices % NBRICK
    tile_keys = jax.random.split(key_tiles, owner_count)
    ordering = jax.vmap(lambda subkey: jax.random.permutation(subkey, TPD))(tile_keys).astype(jnp.int32)
    owner_grp = (group_of[:, None] + shift_grp[ordering]) % NGROUP
    owner_brk = (brick_of[:, None] + shift_brk[ordering]) % NBRICK
    owner_id = owner_grp * NBRICK + owner_brk
    slot_keys = jax.random.split(key_slots, owner_count)
    slotting = jax.vmap(lambda subkey: jax.random.permutation(subkey, TPD))(slot_keys).astype(jnp.int32)
    slot_id = slotting[owner_id, ordering]
    return (owner_id * TPD + slot_id).astype(jnp.int32)


def place_ends(entries, own_key, least, largest):
    longest = entries.shape.index(max(entries.shape))
    spots = []
    for shift in (0, 1):
        where = [jax.random.randint(jax.random.fold_in(own_key, axis), (), 0, length) for axis, length in enumerate(entries.shape)]
        where[longest] = (where[longest] + shift) % entries.shape[longest]
        spots.append(tuple(where))
    return entries.at[spots[0]].set(least).at[spots[1]].set(largest)


def shard_levels(rng, extent, cuts, low, largest):
    factor_of = 1.0
    for position, parts in cuts:
        draws = jax.random.uniform(jax.random.fold_in(jax.random.fold_in(rng, 6), position), (parts,), jnp.float32, low / len(cuts), largest / len(cuts))
        factor_of = factor_of * jnp.repeat(jnp.exp(draws), extent[position] // parts).reshape((-1,) + (1,) * (len(extent) - 1 - position))
    return factor_of


def gaussian(own_key, extent, width, bound, cuts=(), held_as=jnp.bfloat16):
    values = jax.random.normal(own_key, extent, jnp.float32) * width
    if len(cuts) > 0:
        values = shard_levels(own_key, extent, cuts, -0.22, 0.18) * values
    return jnp.clip(values, min=-bound, max=bound).astype(held_as)


def setup_inputs(seed: int = 0) -> dict:
    key_of = jax.random.split(jax.random.key(seed), 8)
    state = gaussian(key_of[0], (NGROUP, FIELDS, NX, BY, BZ), 1.0, 6.0, ((0, 8), (2, 4)), jnp.float32)
    adjoint = gaussian(key_of[1], (NGROUP, FIELDS, NX, BY, BZ), 1.0, 6.0, ((0, 8), (2, 4)), jnp.float32)
    source = gaussian(key_of[2], (NGROUP, FIELDS, NX, BY, BZ), 1.0, 6.0, ((0, 8), (2, 4)), jnp.float32)
    kappa = jnp.clip(jnp.exp(math.log(3.0) - 2.7080502 * jax.random.uniform(key_of[3], (NGROUP, NX, BY, BZ), jnp.float32) ** shard_levels(key_of[3], (NGROUP, NX, BY, BZ), ((0, 8), (1, 4)), -0.2, 0.2)), 0.2, 3.0)
    cut_flags = place_ends((jax.random.randint(key_of[4], (NGROUP, NX, BY, BZ), 0, 3) < 1).astype(jnp.int32), jax.random.fold_in(key_of[4], 1), 0, 1)
    coupling = gaussian(key_of[5], (FIELDS, FIELDS), FIELDS ** -0.5, 2.5, (), jnp.float32)
    target = draw_target(jax.random.fold_in(key_of[7], 71), 0)
    return {"state": state, "adjoint": adjoint, "source": source, "kappa": kappa, "cut_flags": cut_flags, "coupling": coupling, "target": target}


def stencil_apply(values, kappa_cells, coupling):
    padded = jnp.pad(values, ((0, 0), (1, 1), (1, 1), (1, 1)))
    neighbours = padded[:, 2:, 1:-1, 1:-1] + padded[:, :-2, 1:-1, 1:-1]
    neighbours = neighbours + padded[:, 1:-1, 2:, 1:-1] + padded[:, 1:-1, :-2, 1:-1]
    neighbours = neighbours + padded[:, 1:-1, 1:-1, 2:] + padded[:, 1:-1, 1:-1, :-2]
    coupled = jnp.einsum("fg,gxyz->fxyz", coupling.astype(jnp.float32), values.astype(jnp.float32), precision=lax.Precision.HIGHEST)
    return (6.0 + kappa_cells[None]) * values - neighbours + coupled


def reference(state, adjoint, source, kappa, cut_flags, coupling, target):
    fields = state.shape[1]
    cells_x = state.shape[2]
    cells_y = state.shape[3]
    cells_z = state.shape[4]

    def one_group(inputs):
        values, dual, rhs, kappa_cells, flags = inputs
        residual = rhs - stencil_apply(values, kappa_cells, coupling)
        weighted = (1.0 - 0.5 * flags.astype(jnp.float32))[None] * dual * residual
        coarse = weighted.reshape(fields, cells_x // 2, 2, cells_y // 2, 2, cells_z // 2, 2).sum(axis=(2, 4, 6))
        coarse = coarse.reshape(fields, NBRICK, TPD, TILE)
        return coarse.transpose(1, 2, 0, 3)

    pieces = lax.map(one_group, (state, adjoint, source, kappa, cut_flags))
    pieces = pieces.reshape(-1, fields, TILE)
    estimate = jnp.zeros((OWNERS * TPD, fields, TILE), jnp.float32)
    return estimate.at[target.reshape(-1)].set(pieces)
```

```python
import functools
import math

import jax
import jax.numpy as jnp
from jax import lax
from jax.experimental import pallas as pl
from jax.experimental.pallas import tpu as pltpu
from jax.sharding import PartitionSpec as P

F32 = jnp.float32
MESH = pl.DeviceIdType.MESH
PAD = 8
CHUNK = 6


def route_kernel(
    groups, bricks, capacity,
    state, adjoint, source, kappa, flags, coupling, target,
    recv, lookup,
    st, ad, so, ka, fl, acc, packed, outbox, table_v, table_s, slot_v, value_v,
    load_sem, table_sem, halo_send, halo_recv, send_sem, recv_sem,
):
    fields, cells_x, cells_y, lanes = so.shape
    tiles = target.shape[1]
    owners = groups * bricks
    partners = (groups - 1) * bricks
    planes = cells_x // 2
    chunks = cells_x // CHUNK
    per_chunk = CHUNK // 2
    rows = cells_y // 4
    tile_rows = planes * rows // tiles
    grp, brk = lax.axis_index("grp"), lax.axis_index("brk")
    me = grp * bricks + brk

    barrier = pltpu.get_barrier_semaphore()

    def greet(i, carry):
        other = lax.rem(me + i, owners)
        pl.semaphore_signal(
            barrier, inc=1, device_id=(other // bricks, lax.rem(other, bricks)), device_id_type=MESH
        )
        return carry

    def state_load(c):
        return pltpu.make_async_copy(
            state.at[0, :, pl.ds(c * CHUNK, CHUNK)],
            st.at[:, pl.ds(c * CHUNK + 1, CHUNK), pl.ds(PAD, cells_y)],
            load_sem.at[0, c],
        )

    def other_loads(c):
        span = pl.ds(c * CHUNK, CHUNK)
        return (
            pltpu.make_async_copy(adjoint.at[0, :, span], ad.at[:, span], load_sem.at[1, c]),
            pltpu.make_async_copy(source.at[0, :, span], so.at[:, span], load_sem.at[2, c]),
            pltpu.make_async_copy(kappa.at[0, span], ka.at[span], load_sem.at[3, c]),
            pltpu.make_async_copy(flags.at[0, span], fl.at[span], load_sem.at[4, c]),
        )

    state_load(0).start()
    state_load(1).start()
    for c in list(range(1, chunks)) + [0]:
        if 1 <= c < chunks - 1:
            state_load(c + 1).start()
        for copy in other_loads(c):
            copy.start()
    lax.fori_loop(1, owners, greet, 0)

    zeros_pad = jnp.zeros((fields, cells_x + 2, PAD, lanes), F32)
    st[:, :, 0:PAD, :] = zeros_pad
    st[:, :, PAD + cells_y : 2 * PAD + cells_y, :] = zeros_pad
    zeros_face = jnp.zeros((fields, cells_y, lanes), F32)

    @pl.when(brk == 0)
    def _():
        st[:, 0, PAD : PAD + cells_y, :] = zeros_face

    @pl.when(brk == bricks - 1)
    def _():
        st[:, cells_x + 1, PAD : PAD + cells_y, :] = zeros_face

    acc[...] = jnp.zeros_like(acc)

    shift = int(math.log2(tiles))
    earlier = (
        lax.broadcasted_iota(jnp.int32, (tiles, tiles), 0)
        < lax.broadcasted_iota(jnp.int32, (tiles, tiles), 1)
    ).astype(F32).astype(jnp.bfloat16)
    owner_row = lax.broadcasted_iota(jnp.int32, (owners, tiles), 0)
    tile_col = lax.broadcasted_iota(jnp.int32, (owners, tiles), 1)

    def rank_of(chosen):
        return jnp.dot(
            chosen.astype(F32).astype(jnp.bfloat16), earlier, preferred_element_type=F32
        ).astype(jnp.int32)

    mine = lax.shift_right_logical(target[pl.ds(me, 1), :], jnp.int32(shift))
    chosen = jnp.broadcast_to(mine, (owners, tiles)) == owner_row
    rank = rank_of(chosen)
    table = jnp.zeros((owners, tiles), F32)
    for r in range(capacity):
        hit = jnp.logical_and(chosen, rank == r)
        index = jnp.sum(jnp.where(hit, tile_col.astype(F32), 0.0), axis=1, keepdims=True)
        table = jnp.where(tile_col == r, index, table)
    table_v[...] = table.astype(jnp.int32)
    table_copy = pltpu.make_async_copy(table_v, table_s, table_sem)
    table_copy.start()

    coef = [
        [coupling[f, h] + (6.0 if f == h else 0.0) for h in range(fields)] for f in range(fields)
    ]
    lane = lax.broadcasted_iota(jnp.int32, (8, lanes), 1)
    not_first, not_last = lane > 0, lane < lanes - 1
    pair_in = lax.broadcasted_iota(jnp.int32, (2 * lanes, lanes), 0)
    pair_out = lax.broadcasted_iota(jnp.int32, (2 * lanes, lanes), 1)
    pair_sum = (pair_in // 2 == pair_out).astype(F32).astype(jnp.bfloat16)
    count = fields * rows

    def restrict(slot):
        quarter = [acc[slot, pl.ds(q, count, stride=4), :] for q in range(4)]
        both = jnp.concatenate([quarter[0] + quarter[1], quarter[2] + quarter[3]], axis=1)
        high = both.astype(jnp.bfloat16)
        low = (both - high.astype(F32)).astype(jnp.bfloat16)
        return jnp.dot(high, pair_sum, preferred_element_type=F32) + jnp.dot(
            low, pair_sum, preferred_element_type=F32
        )

    def put(plane, result):
        for f in range(fields):
            packed[f, pl.ds(pl.multiple_of(plane * rows, rows), rows), :] = result[
                f * rows : (f + 1) * rows
            ]

    def stencil(plane, slot):
        x = 2 * plane
        for y in range(0, cells_y, 8):
            values = [[st[f, x + i, PAD + y : PAD + y + 8, :] for i in range(4)] for f in range(fields)]
            totals = [None] * fields
            for d in range(2):
                react = ka[x + d, y : y + 8, :]
                weight = 1.0 - 0.5 * fl[x + d, y : y + 8, :].astype(F32)
                for f in range(fields):
                    own = values[f][1 + d]
                    near = values[f][d] + values[f][2 + d]
                    near = near + (
                        st[f, x + 1 + d, PAD + y - 1 : PAD + y + 7, :]
                        + st[f, x + 1 + d, PAD + y + 1 : PAD + y + 9, :]
                    )
                    near = near + (
                        jnp.where(not_first, pltpu.roll(own, 1, 1), 0.0)
                        + jnp.where(not_last, pltpu.roll(own, lanes - 1, 1), 0.0)
                    )
                    mixed = react * own
                    for h in range(fields):
                        mixed = mixed + coef[f][h] * values[h][1 + d]
                    residual = so[f, x + d, y : y + 8, :] - (mixed - near)
                    part = weight * ad[f, x + d, y : y + 8, :] * residual
                    totals[f] = part if d == 0 else totals[f] + part
            for f in range(fields):
                acc[slot, f * cells_y + y : f * cells_y + y + 8, :] = totals[f]

    def step(n, with_state):
        plane = lax.rem(n + per_chunk, planes)
        before = lax.rem(n + per_chunk - 1, planes)

        @pl.when(lax.rem(n, per_chunk) == 0)
        def _():
            c = plane // per_chunk
            if with_state:
                state_load(c + 1).wait()
            for copy in other_loads(c):
                copy.wait()

        result = restrict(lax.rem(n + 1, 2))
        stencil(plane, lax.rem(n, 2))
        put(before, result)

    def steps(start, stop, with_state):
        def body(n, carry):
            step(n, with_state)
            return carry

        lax.fori_loop(start, stop, body, 0)

    state_load(0).wait()
    state_load(1).wait()
    steps(0, per_chunk, True)
    pl.semaphore_wait(barrier, owners - 1)

    inner = pl.ds(PAD, cells_y)
    up = pltpu.make_async_remote_copy(
        src_ref=state.at[0, :, cells_x - 1],
        dst_ref=st.at[:, 0, inner],
        send_sem=halo_send.at[0],
        recv_sem=halo_recv.at[0],
        device_id=(grp, brk + 1),
        device_id_type=MESH,
    )
    down = pltpu.make_async_remote_copy(
        src_ref=state.at[0, :, 0],
        dst_ref=st.at[:, cells_x + 1, inner],
        send_sem=halo_send.at[1],
        recv_sem=halo_recv.at[1],
        device_id=(grp, brk - 1),
        device_id_type=MESH,
    )

    @pl.when(brk < bricks - 1)
    def _():
        up.start()

    @pl.when(brk > 0)
    def _():
        down.start()

    steps(per_chunk, planes - 2 * per_chunk, True)

    @pl.when(brk > 0)
    def _():
        up.wait_recv()
        down.wait_send()

    @pl.when(brk < bricks - 1)
    def _():
        down.wait_recv()
        up.wait_send()

    steps(planes - 2 * per_chunk, planes, False)
    put(per_chunk - 1, restrict((planes - 1) % 2))
    table_copy.wait()

    def outgoing(p):
        ahead = p // bricks + 1
        to_grp, to_brk = lax.rem(grp + ahead, groups), lax.rem(p, bricks)
        place = (ahead - 1) * bricks + brk
        return to_grp * bricks + to_brk, pltpu.make_async_remote_copy(
            src_ref=outbox.at[p],
            dst_ref=recv.at[place],
            send_sem=send_sem.at[p],
            recv_sem=recv_sem.at[place],
            device_id=(to_grp, to_brk),
            device_id_type=MESH,
        )

    def send(p, carry):
        owner, copy = outgoing(p)
        for r in range(capacity):
            t = jnp.clip(table_s[owner, r], 0, tiles - 1)
            for f in range(fields):
                for k in range(tile_rows):
                    outbox[p, (r * fields + f) * tile_rows + k, :, :] = packed[
                        f, pl.ds(t * tile_rows + k, 1), :
                    ]
        copy.start()
        return carry

    lax.fori_loop(0, partners, send, 0)

    every = target[...]
    arriving = lax.shift_right_logical(every, jnp.int32(shift)) == me
    sender_grp = lax.shift_right_logical(owner_row, jnp.int32(int(math.log2(bricks))))
    sender_brk = jnp.bitwise_and(owner_row, bricks - 1)
    ahead = grp - sender_grp
    ahead = jnp.where(ahead < 0, ahead + groups, ahead)
    position = ((ahead - 1) * bricks + sender_brk) * capacity + rank_of(arriving)
    value_v[...] = jnp.where(arriving, position, 0).astype(F32)
    slot_v[...] = jnp.where(arriving, jnp.bitwise_and(every, tiles - 1), -1)
    down_iota = lax.broadcasted_iota(jnp.int32, (tiles, tiles), 0)
    across_iota = lax.broadcasted_iota(jnp.int32, (tiles, tiles), 1)

    def find(s, found):
        slots = jnp.broadcast_to(slot_v[pl.ds(s, 1), :], (tiles, tiles))
        values = jnp.broadcast_to(value_v[pl.ds(s, 1), :], (tiles, tiles))
        return found + jnp.where(slots == down_iota, values, 0.0)

    found = lax.fori_loop(0, owners, find, jnp.zeros((tiles, tiles), F32))
    column = jnp.sum(found, axis=1, keepdims=True)
    line = jnp.sum(jnp.where(down_iota == across_iota, column, 0.0), axis=0, keepdims=True)
    lookup[...] = line.astype(jnp.int32)

    def finish(p, carry):
        _, copy = outgoing(p)
        copy.wait_send()
        pltpu.make_async_remote_copy(
            src_ref=outbox.at[p],
            dst_ref=recv.at[p],
            send_sem=send_sem.at[p],
            recv_sem=recv_sem.at[p],
            device_id=(lax.rem(grp + 1, groups), brk),
            device_id_type=MESH,
        ).wait_recv()
        return carry

    lax.fori_loop(0, partners, finish, 0)


def place_kernel(lookup, received, out, stage):
    fields, tiles, length = out.shape
    lanes = received.shape[-1]
    tile_rows = length // lanes

    def body(i, carry):
        for u in range(8):
            j = i * 8 + u
            base = jnp.clip(lookup[0, j], 0, received.shape[0] // (fields * tile_rows) - 1)
            base = base * (fields * tile_rows)
            for f in range(fields):
                for k in range(tile_rows):
                    stage[f * tile_rows + k, pl.ds(j, 1), :] = received[base + f * tile_rows + k]
        return carry

    lax.fori_loop(0, tiles // 8, body, 0)
    for f in range(fields):
        for k in range(tile_rows):
            out[f, :, k * lanes : (k + 1) * lanes] = stage[f * tile_rows + k]


def local(groups, bricks, state, adjoint, source, kappa, cut_flags, coupling, target):
    _, fields, cells_x, cells_y, lanes = state.shape
    tiles = target.shape[1]
    owners = groups * bricks
    partners = (groups - 1) * bricks
    capacity = tiles // partners + 1
    planes = cells_x // 2
    rows = cells_y // 4
    length = planes * rows * lanes // tiles
    tile_rows = length // lanes
    block = capacity * fields * tile_rows
    chunks = cells_x // CHUNK
    hbm = pl.BlockSpec(memory_space=pl.ANY)
    vmem = pl.BlockSpec(memory_space=pltpu.VMEM)
    smem = pl.BlockSpec(memory_space=pltpu.SMEM)
    brick = (fields, cells_x, cells_y, lanes)
    cells = math.prod(brick)
    received, lookup = pl.pallas_call(
        functools.partial(route_kernel, groups, bricks, capacity),
        out_shape=(
            jax.ShapeDtypeStruct((partners, block, 1, lanes), F32),
            jax.ShapeDtypeStruct((1, tiles), jnp.int32),
        ),
        in_specs=[hbm, hbm, hbm, hbm, hbm, smem, vmem],
        out_specs=(hbm, vmem),
        scratch_shapes=[
            pltpu.VMEM((fields, cells_x + 2, cells_y + 2 * PAD, lanes), F32),
            pltpu.VMEM(brick, F32),
            pltpu.VMEM(brick, F32),
            pltpu.VMEM(brick[1:], F32),
            pltpu.VMEM(brick[1:], jnp.int32),
            pltpu.VMEM((2, fields * cells_y + 8, lanes), F32),
            pltpu.VMEM((fields, planes * rows, lanes), F32),
            pltpu.VMEM((partners, block, 1, lanes), F32),
            pltpu.VMEM((owners, tiles), jnp.int32),
            pltpu.SMEM((owners, tiles), jnp.int32),
            pltpu.VMEM((owners, tiles), jnp.int32),
            pltpu.VMEM((owners, tiles), F32),
            pltpu.SemaphoreType.DMA((5, chunks)),
            pltpu.SemaphoreType.DMA,
            pltpu.SemaphoreType.DMA((2,)),
            pltpu.SemaphoreType.DMA((2,)),
            pltpu.SemaphoreType.DMA((partners,)),
            pltpu.SemaphoreType.DMA((partners,)),
        ],
        compiler_params=pltpu.CompilerParams(
            collective_id=0, has_side_effects=True, vmem_limit_bytes=56 * 1024 * 1024
        ),
        cost_estimate=pl.CostEstimate(flops=25 * cells, bytes_accessed=14 * cells, transcendentals=0),
    )(state, adjoint, source, kappa, cut_flags, coupling, target)
    received = received.reshape(partners * block, 1, lanes)
    placed = pl.pallas_call(
        place_kernel,
        out_shape=jax.ShapeDtypeStruct((fields, tiles, length), F32),
        in_specs=[smem, vmem],
        out_specs=vmem,
        scratch_shapes=[pltpu.VMEM((fields * tile_rows, tiles, lanes), F32)],
        compiler_params=pltpu.CompilerParams(vmem_limit_bytes=24 * 1024 * 1024),
    )(lookup, received)
    return placed.transpose(1, 0, 2)


def solution(mesh):
    placed = (
        P("grp", None, "brk", None, None),
        P("grp", None, "brk", None, None),
        P("grp", None, "brk", None, None),
        P("grp", "brk", None, None),
        P("grp", "brk", None, None),
        P(),
        P(),
    )
    return jax.shard_map(
        functools.partial(local, mesh.shape["grp"], mesh.shape["brk"]),
        mesh=mesh, in_specs=placed, out_specs=P(("grp", "brk"), None, None), check_vma=False,
    )
```

```python
import functools
import math

import jax
import jax.numpy as jnp
from jax import lax
from jax.experimental import pallas as pl
from jax.experimental.pallas import tpu as pltpu
from jax.sharding import PartitionSpec as P

F32 = jnp.float32
MESH = pl.DeviceIdType.MESH
PAD = 8
CHUNK = 6


def split_fields(fields):
    first = list(range(0, 1))
    rest = list(range(1, fields))
    half = (len(rest) + 1) // 2
    return [part for part in (first, rest[:half], rest[half:]) if part]


def route_kernel(
    groups, bricks, capacity, phases,
    state, adjoint, source, kappa, flags, coupling, target,
    out, *scratch,
):
    stages = len(phases)
    outbox, recv = scratch[:stages], scratch[stages : 2 * stages]
    (
        st, ad, so, ka, fl, acc, packed, table_v, table_s, slot_v, value_v, line_v, line_s, stage,
        load_sem, late_sem, table_sem, line_sem, halo_send, halo_recv, send_sem, recv_sem,
    ) = scratch[2 * stages :]
    fields, cells_x, cells_y, lanes = so.shape
    tiles = target.shape[1]
    owners = groups * bricks
    partners = (groups - 1) * bricks
    planes = cells_x // 2
    chunks = cells_x // CHUNK
    per_chunk = CHUNK // 2
    rows = cells_y // 4
    tile_rows = planes * rows // tiles
    grp, brk = lax.axis_index("grp"), lax.axis_index("brk")
    me = grp * bricks + brk

    barrier = pltpu.get_barrier_semaphore()

    def greet(i, carry):
        other = lax.rem(me + i, owners)
        pl.semaphore_signal(
            barrier, inc=1, device_id=(other // bricks, lax.rem(other, bricks)), device_id_type=MESH
        )
        return carry

    def state_load(c):
        return pltpu.make_async_copy(
            state.at[0, :, pl.ds(c * CHUNK, CHUNK)],
            st.at[:, pl.ds(c * CHUNK + 1, CHUNK), pl.ds(PAD, cells_y)],
            load_sem.at[0, c],
        )

    def other_loads(c):
        span = pl.ds(c * CHUNK, CHUNK)
        here = pl.ds(phases[0][0], len(phases[0]))
        return (
            pltpu.make_async_copy(adjoint.at[0, here, span], ad.at[here, span], load_sem.at[1, c]),
            pltpu.make_async_copy(source.at[0, here, span], so.at[here, span], load_sem.at[2, c]),
            pltpu.make_async_copy(kappa.at[0, span], ka.at[span], load_sem.at[3, c]),
            pltpu.make_async_copy(flags.at[0, span], fl.at[span], load_sem.at[4, c]),
        )

    def late_loads(i):
        here = pl.ds(phases[i][0], len(phases[i]))
        return (
            pltpu.make_async_copy(adjoint.at[0, here], ad.at[here], late_sem.at[0, i]),
            pltpu.make_async_copy(source.at[0, here], so.at[here], late_sem.at[1, i]),
        )

    state_load(0).start()
    state_load(1).start()
    for c in list(range(1, chunks)) + [0]:
        if 1 <= c < chunks - 1:
            state_load(c + 1).start()
        for copy in other_loads(c):
            copy.start()
    for i in range(1, stages):
        for copy in late_loads(i):
            copy.start()
    lax.fori_loop(1, owners, greet, 0)

    zeros_pad = jnp.zeros((fields, cells_x + 2, PAD, lanes), F32)
    st[:, :, 0:PAD, :] = zeros_pad
    st[:, :, PAD + cells_y : 2 * PAD + cells_y, :] = zeros_pad
    zeros_face = jnp.zeros((fields, cells_y, lanes), F32)

    @pl.when(brk == 0)
    def _():
        st[:, 0, PAD : PAD + cells_y, :] = zeros_face

    @pl.when(brk == bricks - 1)
    def _():
        st[:, cells_x + 1, PAD : PAD + cells_y, :] = zeros_face

    acc[...] = jnp.zeros_like(acc)

    shift = int(math.log2(tiles))
    earlier = (
        lax.broadcasted_iota(jnp.int32, (tiles, tiles), 0)
        < lax.broadcasted_iota(jnp.int32, (tiles, tiles), 1)
    ).astype(F32).astype(jnp.bfloat16)
    owner_row = lax.broadcasted_iota(jnp.int32, (owners, tiles), 0)
    tile_col = lax.broadcasted_iota(jnp.int32, (owners, tiles), 1)

    def rank_of(chosen):
        return jnp.dot(
            chosen.astype(F32).astype(jnp.bfloat16), earlier, preferred_element_type=F32
        ).astype(jnp.int32)

    mine = lax.shift_right_logical(target[pl.ds(me, 1), :], jnp.int32(shift))
    chosen = jnp.broadcast_to(mine, (owners, tiles)) == owner_row
    rank = rank_of(chosen)
    table = jnp.zeros((owners, tiles), F32)
    for r in range(capacity):
        hit = jnp.logical_and(chosen, rank == r)
        index = jnp.sum(jnp.where(hit, tile_col.astype(F32), 0.0), axis=1, keepdims=True)
        table = jnp.where(tile_col == r, index, table)
    table_v[...] = table.astype(jnp.int32)
    table_copy = pltpu.make_async_copy(table_v, table_s, table_sem)
    table_copy.start()

    coef = [
        [coupling[f, h] + (6.0 if f == h else 0.0) for h in range(fields)] for f in range(fields)
    ]
    lane = lax.broadcasted_iota(jnp.int32, (8, lanes), 1)
    not_first, not_last = lane > 0, lane < lanes - 1
    pair_in = lax.broadcasted_iota(jnp.int32, (2 * lanes, lanes), 0)
    pair_out = lax.broadcasted_iota(jnp.int32, (2 * lanes, lanes), 1)
    pair_sum = (pair_in // 2 == pair_out).astype(F32).astype(jnp.bfloat16)
    def restrict(slot, fs):
        count = len(fs) * rows
        quarter = [acc[slot, pl.ds(q, count, stride=4), :] for q in range(4)]
        both = jnp.concatenate([quarter[0] + quarter[1], quarter[2] + quarter[3]], axis=1)
        high = both.astype(jnp.bfloat16)
        low = (both - high.astype(F32)).astype(jnp.bfloat16)
        return jnp.dot(high, pair_sum, preferred_element_type=F32) + jnp.dot(
            low, pair_sum, preferred_element_type=F32
        )

    def put(plane, result, fs):
        for i, f in enumerate(fs):
            packed[f, pl.ds(pl.multiple_of(plane * rows, rows), rows), :] = result[
                i * rows : (i + 1) * rows
            ]

    def stencil(plane, slot, fs):
        x = 2 * plane
        for y in range(0, cells_y, 8):
            inside = slice(PAD + y, PAD + y + 8)
            centre = [[st[f, x + 1 + d, inside, :] for d in range(2)] for f in range(fields)]
            totals = [None] * len(fs)
            for d in range(2):
                react = ka[x + d, y : y + 8, :]
                weight = 1.0 - 0.5 * fl[x + d, y : y + 8, :].astype(F32)
                for i, f in enumerate(fs):
                    own = centre[f][d]
                    near = centre[f][1 - d] + st[f, x + 3 * d, inside, :]
                    near = near + (
                        st[f, x + 1 + d, PAD + y - 1 : PAD + y + 7, :]
                        + st[f, x + 1 + d, PAD + y + 1 : PAD + y + 9, :]
                    )
                    near = near + (
                        jnp.where(not_first, pltpu.roll(own, 1, 1), 0.0)
                        + jnp.where(not_last, pltpu.roll(own, lanes - 1, 1), 0.0)
                    )
                    mixed = react * own
                    for h in range(fields):
                        mixed = mixed + coef[f][h] * centre[h][d]
                    residual = so[f, x + d, y : y + 8, :] - (mixed - near)
                    part = weight * ad[f, x + d, y : y + 8, :] * residual
                    totals[i] = part if d == 0 else totals[i] + part
            for i in range(len(fs)):
                acc[slot, i * cells_y + y : i * cells_y + y + 8, :] = totals[i]

    def steps(start, stop, fs, with_loads, with_state):
        def body(n, carry):
            plane = lax.rem(n + per_chunk, planes)
            before = lax.rem(n + per_chunk - 1, planes)
            if with_loads:

                @pl.when(lax.rem(n, per_chunk) == 0)
                def _():
                    c = plane // per_chunk
                    if with_state:
                        state_load(c + 1).wait()
                    for copy in other_loads(c):
                        copy.wait()

            result = restrict(lax.rem(n + 1, 2), fs)
            stencil(plane, lax.rem(n, 2), fs)
            put(before, result, fs)
            return carry

        lax.fori_loop(start, stop, body, 0)

    inner = pl.ds(PAD, cells_y)

    def faces(i):
        here = pl.ds(phases[i][0], len(phases[i]))
        up = pltpu.make_async_remote_copy(
            src_ref=state.at[0, here, cells_x - 1],
            dst_ref=st.at[here, 0, inner],
            send_sem=halo_send.at[0, i],
            recv_sem=halo_recv.at[0, i],
            device_id=(grp, brk + 1),
            device_id_type=MESH,
        )
        down = pltpu.make_async_remote_copy(
            src_ref=state.at[0, here, 0],
            dst_ref=st.at[here, cells_x + 1, inner],
            send_sem=halo_send.at[1, i],
            recv_sem=halo_recv.at[1, i],
            device_id=(grp, brk - 1),
            device_id_type=MESH,
        )
        return up, down

    def start_faces():
        for i in range(stages):
            up, down = faces(i)

            @pl.when(brk < bricks - 1)
            def _():
                up.start()

            @pl.when(brk > 0)
            def _():
                down.start()

    def wait_faces(i):
        up, down = faces(i)

        @pl.when(brk > 0)
        def _():
            up.wait_recv()
            down.wait_send()

        @pl.when(brk < bricks - 1)
        def _():
            down.wait_recv()
            up.wait_send()

    def outgoing(i, p):
        ahead = p // bricks + 1
        to_grp, to_brk = lax.rem(grp + ahead, groups), lax.rem(p, bricks)
        place = (ahead - 1) * bricks + brk
        return to_grp * bricks + to_brk, pltpu.make_async_remote_copy(
            src_ref=outbox[i].at[p],
            dst_ref=recv[i].at[place],
            send_sem=send_sem.at[i, p],
            recv_sem=recv_sem.at[i, place],
            device_id=(to_grp, to_brk),
            device_id_type=MESH,
        )

    def send_all(i, fs):
        def send(p, carry):
            owner, copy = outgoing(i, p)
            for r in range(capacity):
                t = jnp.clip(table_s[owner, r], 0, tiles - 1) * tile_rows
                for j, f in enumerate(fs):
                    for k in range(tile_rows):
                        outbox[i][p, (r * len(fs) + j) * tile_rows + k, :, :] = packed[
                            f, pl.ds(t + k, 1), :
                        ]
            copy.start()
            return carry

        lax.fori_loop(0, partners, send, 0)

    for i, fs in enumerate(phases):
        if i == 0:
            state_load(0).wait()
            state_load(1).wait()
            steps(0, per_chunk, fs, True, True)
            pl.semaphore_wait(barrier, owners - 1)
            start_faces()
            steps(per_chunk, planes - 2 * per_chunk, fs, True, True)
            wait_faces(0)
            steps(planes - 2 * per_chunk, planes, fs, True, False)
            table_copy.wait()
        else:
            for copy in late_loads(i):
                copy.wait()
            wait_faces(i)
            steps(0, planes, fs, False, False)
        put(per_chunk - 1, restrict((planes - 1) % 2, fs), fs)
        send_all(i, fs)

    every = target[...]
    arriving = lax.shift_right_logical(every, jnp.int32(shift)) == me
    sender_grp = lax.shift_right_logical(owner_row, jnp.int32(int(math.log2(bricks))))
    sender_brk = jnp.bitwise_and(owner_row, bricks - 1)
    ahead = grp - sender_grp
    ahead = jnp.where(ahead < 0, ahead + groups, ahead)
    position = ((ahead - 1) * bricks + sender_brk) * capacity + rank_of(arriving)
    value_v[...] = jnp.where(arriving, position, 0).astype(F32)
    slot_v[...] = jnp.where(arriving, jnp.bitwise_and(every, tiles - 1), -1)
    down_iota = lax.broadcasted_iota(jnp.int32, (tiles, tiles), 0)
    across_iota = lax.broadcasted_iota(jnp.int32, (tiles, tiles), 1)

    def find(s, found):
        slots = jnp.broadcast_to(slot_v[pl.ds(s, 1), :], (tiles, tiles))
        values = jnp.broadcast_to(value_v[pl.ds(s, 1), :], (tiles, tiles))
        return found + jnp.where(slots == down_iota, values, 0.0)

    found = lax.fori_loop(0, owners, find, jnp.zeros((tiles, tiles), F32))
    column = jnp.sum(found, axis=1, keepdims=True)
    line = jnp.sum(jnp.where(down_iota == across_iota, column, 0.0), axis=0, keepdims=True)
    line_v[...] = line.astype(jnp.int32)
    line_copy = pltpu.make_async_copy(line_v, line_s, line_sem)
    line_copy.start()
    line_copy.wait()

    for i, fs in enumerate(phases):

        def arrive(p, carry):
            pltpu.make_async_remote_copy(
                src_ref=outbox[i].at[p],
                dst_ref=recv[i].at[p],
                send_sem=send_sem.at[i, p],
                recv_sem=recv_sem.at[i, p],
                device_id=(lax.rem(grp + 1, groups), brk),
                device_id_type=MESH,
            ).wait_recv()
            return carry

        lax.fori_loop(0, partners, arrive, 0)
        block = len(fs) * tile_rows

        def place_tiles(n, carry):
            for u in range(8):
                slot = n * 8 + u
                at = jnp.clip(line_s[0, slot], 0, partners * capacity - 1)
                box, first = at // capacity, lax.rem(at, capacity) * block
                for j in range(block):
                    stage[j, pl.ds(slot, 1), :] = recv[i][box, first + j, :, :]
            return carry

        lax.fori_loop(0, tiles // 8, place_tiles, 0)
        for j, f in enumerate(fs):
            for k in range(tile_rows):
                out[f, :, k * lanes : (k + 1) * lanes] = stage[j * tile_rows + k]

    for i in range(stages):

        def sent(p, carry):
            outgoing(i, p)[1].wait_send()
            return carry

        lax.fori_loop(0, partners, sent, 0)


def local(groups, bricks, state, adjoint, source, kappa, cut_flags, coupling, target):
    _, fields, cells_x, cells_y, lanes = state.shape
    tiles = target.shape[1]
    owners = groups * bricks
    partners = (groups - 1) * bricks
    capacity = tiles // partners + 1
    planes = cells_x // 2
    rows = cells_y // 4
    length = planes * rows * lanes // tiles
    tile_rows = length // lanes
    chunks = cells_x // CHUNK
    phases = split_fields(fields)
    stages = len(phases)
    widest = max(len(fs) for fs in phases)
    hbm = pl.BlockSpec(memory_space=pl.ANY)
    vmem = pl.BlockSpec(memory_space=pltpu.VMEM)
    smem = pl.BlockSpec(memory_space=pltpu.SMEM)
    brick = (fields, cells_x, cells_y, lanes)
    cells = math.prod(brick)
    boxes = [
        pltpu.VMEM((partners, capacity * len(fs) * tile_rows, 1, lanes), F32) for fs in phases
    ]
    placed = pl.pallas_call(
        functools.partial(route_kernel, groups, bricks, capacity, phases),
        out_shape=jax.ShapeDtypeStruct((fields, tiles, length), F32),
        in_specs=[hbm, hbm, hbm, hbm, hbm, smem, vmem],
        out_specs=vmem,
        scratch_shapes=boxes + boxes + [
            pltpu.VMEM((fields, cells_x + 2, cells_y + 2 * PAD, lanes), F32),
            pltpu.VMEM(brick, F32),
            pltpu.VMEM(brick, F32),
            pltpu.VMEM(brick[1:], F32),
            pltpu.VMEM(brick[1:], jnp.int32),
            pltpu.VMEM((2, widest * cells_y + 8, lanes), F32),
            pltpu.VMEM((fields, planes * rows, lanes), F32),
            pltpu.VMEM((owners, tiles), jnp.int32),
            pltpu.SMEM((owners, tiles), jnp.int32),
            pltpu.VMEM((owners, tiles), jnp.int32),
            pltpu.VMEM((owners, tiles), F32),
            pltpu.VMEM((1, tiles), jnp.int32),
            pltpu.SMEM((1, tiles), jnp.int32),
            pltpu.VMEM((widest * tile_rows, tiles, lanes), F32),
            pltpu.SemaphoreType.DMA((5, chunks)),
            pltpu.SemaphoreType.DMA((2, stages)),
            pltpu.SemaphoreType.DMA,
            pltpu.SemaphoreType.DMA,
            pltpu.SemaphoreType.DMA((2, stages)),
            pltpu.SemaphoreType.DMA((2, stages)),
            pltpu.SemaphoreType.DMA((stages, partners)),
            pltpu.SemaphoreType.DMA((stages, partners)),
        ],
        compiler_params=pltpu.CompilerParams(
            collective_id=0, has_side_effects=True, vmem_limit_bytes=56 * 1024 * 1024
        ),
        cost_estimate=pl.CostEstimate(flops=25 * cells, bytes_accessed=14 * cells, transcendentals=0),
    )(state, adjoint, source, kappa, cut_flags, coupling, target)
    return placed.transpose(1, 0, 2)


def solution(mesh):
    placed = (
        P("grp", None, "brk", None, None),
        P("grp", None, "brk", None, None),
        P("grp", None, "brk", None, None),
        P("grp", "brk", None, None),
        P("grp", "brk", None, None),
        P(),
        P(),
    )
    return jax.shard_map(
        functools.partial(local, mesh.shape["grp"], mesh.shape["brk"]),
        mesh=mesh, in_specs=placed, out_specs=P(("grp", "brk"), None, None), check_vma=False,
    )
```

```python
import functools
import math

import jax
import jax.numpy as jnp
from jax import lax
from jax.experimental import pallas as pl
from jax.experimental.pallas import tpu as pltpu
from jax.sharding import PartitionSpec as P

F32 = jnp.float32
MESH = pl.DeviceIdType.MESH
PAD = 8
CHUNK = 6


def split_fields(fields):
    first = list(range(0, 1))
    rest = list(range(1, fields))
    half = (len(rest) + 1) // 2
    return [part for part in (first, rest[:half], rest[half:]) if part]


def route_kernel(
    groups, bricks, capacity, phases,
    state, adjoint, source, kappa, flags, coupling, target,
    out, *scratch,
):
    stages = len(phases)
    outbox, recv = scratch[:stages], scratch[stages : 2 * stages]
    (
        st, ad, so, ka, fl, acc, packed, table_v, table_s, slot_v, value_v, line_v, line_s, stage,
        load_sem, late_sem, table_sem, line_sem, halo_send, halo_recv, send_sem, recv_sem,
    ) = scratch[2 * stages :]
    fields, cells_x, cells_y, lanes = so.shape
    tiles = target.shape[1]
    owners = groups * bricks
    partners = (groups - 1) * bricks
    planes = cells_x // 2
    chunks = cells_x // CHUNK
    per_chunk = CHUNK // 2
    rows = cells_y // 4
    tile_rows = planes * rows // tiles
    grp, brk = lax.axis_index("grp"), lax.axis_index("brk")
    me = grp * bricks + brk

    barrier = pltpu.get_barrier_semaphore()

    def greet(i, carry):
        other = lax.rem(me + i, owners)
        pl.semaphore_signal(
            barrier, inc=1, device_id=(other // bricks, lax.rem(other, bricks)), device_id_type=MESH
        )
        return carry

    def state_load(c):
        return pltpu.make_async_copy(
            state.at[0, :, pl.ds(c * CHUNK, CHUNK)],
            st.at[:, pl.ds(c * CHUNK + 1, CHUNK), pl.ds(PAD, cells_y)],
            load_sem.at[0, c],
        )

    def other_loads(c):
        span = pl.ds(c * CHUNK, CHUNK)
        here = pl.ds(phases[0][0], len(phases[0]))
        return (
            pltpu.make_async_copy(adjoint.at[0, here, span], ad.at[here, span], load_sem.at[1, c]),
            pltpu.make_async_copy(source.at[0, here, span], so.at[here, span], load_sem.at[2, c]),
            pltpu.make_async_copy(kappa.at[0, span], ka.at[span], load_sem.at[3, c]),
            pltpu.make_async_copy(flags.at[0, span], fl.at[span], load_sem.at[4, c]),
        )

    def late_loads(i):
        here = pl.ds(phases[i][0], len(phases[i]))
        return (
            pltpu.make_async_copy(adjoint.at[0, here], ad.at[here], late_sem.at[0, i]),
            pltpu.make_async_copy(source.at[0, here], so.at[here], late_sem.at[1, i]),
        )

    state_load(0).start()
    state_load(1).start()
    for c in list(range(1, chunks)) + [0]:
        if 1 <= c < chunks - 1:
            state_load(c + 1).start()
        for copy in other_loads(c):
            copy.start()
    for i in range(1, stages):
        for copy in late_loads(i):
            copy.start()
    lax.fori_loop(1, owners, greet, 0)

    zeros_pad = jnp.zeros((fields, cells_x + 2, PAD, lanes), F32)
    st[:, :, 0:PAD, :] = zeros_pad
    st[:, :, PAD + cells_y : 2 * PAD + cells_y, :] = zeros_pad
    zeros_face = jnp.zeros((fields, cells_y, lanes), F32)

    @pl.when(brk == 0)
    def _():
        st[:, 0, PAD : PAD + cells_y, :] = zeros_face

    @pl.when(brk == bricks - 1)
    def _():
        st[:, cells_x + 1, PAD : PAD + cells_y, :] = zeros_face

    shift = int(math.log2(tiles))
    earlier = (
        lax.broadcasted_iota(jnp.int32, (tiles, tiles), 0)
        < lax.broadcasted_iota(jnp.int32, (tiles, tiles), 1)
    ).astype(F32).astype(jnp.bfloat16)
    owner_row = lax.broadcasted_iota(jnp.int32, (owners, tiles), 0)
    tile_col = lax.broadcasted_iota(jnp.int32, (owners, tiles), 1)

    def rank_of(chosen):
        return jnp.dot(
            chosen.astype(F32).astype(jnp.bfloat16), earlier, preferred_element_type=F32
        ).astype(jnp.int32)

    mine = lax.shift_right_logical(target[pl.ds(me, 1), :], jnp.int32(shift))
    chosen = jnp.broadcast_to(mine, (owners, tiles)) == owner_row
    rank = rank_of(chosen)
    table = jnp.zeros((owners, tiles), F32)
    for r in range(capacity):
        hit = jnp.logical_and(chosen, rank == r)
        index = jnp.sum(jnp.where(hit, tile_col.astype(F32), 0.0), axis=1, keepdims=True)
        table = jnp.where(tile_col == r, index, table)
    table_v[...] = table.astype(jnp.int32)
    table_copy = pltpu.make_async_copy(table_v, table_s, table_sem)
    table_copy.start()

    coef = [
        [coupling[f, h] + (6.0 if f == h else 0.0) for h in range(fields)] for f in range(fields)
    ]
    lane = lax.broadcasted_iota(jnp.int32, (8, lanes), 1)
    not_first, not_last = lane > 0, lane < lanes - 1
    most = max(len(fs) for fs in phases) * rows
    spot = lax.broadcasted_iota(jnp.int32, (most, lanes), 1)
    even_lane = jnp.bitwise_and(spot, 1) == 0
    half = lanes // 2
    order = jnp.where(spot < half, 2 * spot, 2 * (spot - half) + 1)

    def restrict(plane, fs):
        count = len(fs) * rows
        quarter = [acc[plane, pl.ds(q, count, stride=4), :] for q in range(4)]
        first, second = quarter[0] + quarter[1], quarter[2] + quarter[3]
        first = first + pltpu.roll(first, lanes - 1, 1)
        second = second + pltpu.roll(second, 1, 1)
        mixed = jnp.where(even_lane[:count], first, second)
        result = jnp.take_along_axis(mixed, order[:count], axis=1, mode="promise_in_bounds")
        for i, f in enumerate(fs):
            packed[f, pl.ds(pl.multiple_of(plane * rows, rows), rows), :] = result[
                i * rows : (i + 1) * rows
            ]

    def restrict_all(fs):
        def body(n, carry):
            for u in range(4):
                restrict(n * 4 + u, fs)
            return carry

        lax.fori_loop(0, planes // 4, body, 0)

    def stencil(plane, fs):
        x = 2 * plane
        for y in range(0, cells_y, 8):
            inside = slice(PAD + y, PAD + y + 8)
            centre = [[st[f, x + 1 + d, inside, :] for d in range(2)] for f in range(fields)]
            totals = [None] * len(fs)
            for d in range(2):
                react = ka[x + d, y : y + 8, :]
                weight = 1.0 - 0.5 * fl[x + d, y : y + 8, :].astype(F32)
                for i, f in enumerate(fs):
                    own = centre[f][d]
                    near = centre[f][1 - d] + st[f, x + 3 * d, inside, :]
                    near = near + (
                        st[f, x + 1 + d, PAD + y - 1 : PAD + y + 7, :]
                        + st[f, x + 1 + d, PAD + y + 1 : PAD + y + 9, :]
                    )
                    near = near + (
                        jnp.where(not_first, pltpu.roll(own, 1, 1), 0.0)
                        + jnp.where(not_last, pltpu.roll(own, lanes - 1, 1), 0.0)
                    )
                    mixed = react * own
                    for h in range(fields):
                        mixed = mixed + coef[f][h] * centre[h][d]
                    residual = so[f, x + d, y : y + 8, :] - (mixed - near)
                    part = weight * ad[f, x + d, y : y + 8, :] * residual
                    totals[i] = part if d == 0 else totals[i] + part
            for i in range(len(fs)):
                acc[plane, i * cells_y + y : i * cells_y + y + 8, :] = totals[i]

    def steps(start, stop, fs, with_loads, with_state):
        def body(n, carry):
            c = lax.rem(n + 1, chunks)
            if with_loads:
                if with_state:
                    state_load(c + 1).wait()
                for copy in other_loads(c):
                    copy.wait()
            for u in range(per_chunk):
                stencil(c * per_chunk + u, fs)
            return carry

        lax.fori_loop(start, stop, body, 0)

    inner = pl.ds(PAD, cells_y)

    def faces(i):
        here = pl.ds(phases[i][0], len(phases[i]))
        up = pltpu.make_async_remote_copy(
            src_ref=state.at[0, here, cells_x - 1],
            dst_ref=st.at[here, 0, inner],
            send_sem=halo_send.at[0, i],
            recv_sem=halo_recv.at[0, i],
            device_id=(grp, brk + 1),
            device_id_type=MESH,
        )
        down = pltpu.make_async_remote_copy(
            src_ref=state.at[0, here, 0],
            dst_ref=st.at[here, cells_x + 1, inner],
            send_sem=halo_send.at[1, i],
            recv_sem=halo_recv.at[1, i],
            device_id=(grp, brk - 1),
            device_id_type=MESH,
        )
        return up, down

    def start_faces():
        for i in range(stages):
            up, down = faces(i)

            @pl.when(brk < bricks - 1)
            def _():
                up.start()

            @pl.when(brk > 0)
            def _():
                down.start()

    def wait_faces(i):
        up, down = faces(i)

        @pl.when(brk > 0)
        def _():
            up.wait_recv()
            down.wait_send()

        @pl.when(brk < bricks - 1)
        def _():
            down.wait_recv()
            up.wait_send()

    def outgoing(i, p):
        ahead = p // bricks + 1
        to_grp, to_brk = lax.rem(grp + ahead, groups), lax.rem(p, bricks)
        place = (ahead - 1) * bricks + brk
        return to_grp * bricks + to_brk, pltpu.make_async_remote_copy(
            src_ref=outbox[i].at[p],
            dst_ref=recv[i].at[place],
            send_sem=send_sem.at[i, p],
            recv_sem=recv_sem.at[i, place],
            device_id=(to_grp, to_brk),
            device_id_type=MESH,
        )

    def send_all(i, fs):
        def send(p, carry):
            owner, copy = outgoing(i, p)
            for r in range(capacity):
                t = jnp.clip(table_s[owner, r], 0, tiles - 1) * tile_rows
                for j, f in enumerate(fs):
                    for k in range(tile_rows):
                        outbox[i][p, (r * len(fs) + j) * tile_rows + k, :, :] = packed[
                            f, pl.ds(t + k, 1), :
                        ]
            copy.start()
            return carry

        lax.fori_loop(0, partners, send, 0)

    for i, fs in enumerate(phases):
        if i == 0:
            state_load(0).wait()
            state_load(1).wait()
            steps(0, 1, fs, True, True)
            pl.semaphore_wait(barrier, owners - 1)
            start_faces()
            steps(1, chunks - 2, fs, True, True)
            wait_faces(0)
            steps(chunks - 2, chunks, fs, True, False)
            table_copy.wait()
        else:
            for copy in late_loads(i):
                copy.wait()
            wait_faces(i)
            steps(0, chunks, fs, False, False)
        restrict_all(fs)
        send_all(i, fs)

    every = target[...]
    arriving = lax.shift_right_logical(every, jnp.int32(shift)) == me
    sender_grp = lax.shift_right_logical(owner_row, jnp.int32(int(math.log2(bricks))))
    sender_brk = jnp.bitwise_and(owner_row, bricks - 1)
    ahead = grp - sender_grp
    ahead = jnp.where(ahead < 0, ahead + groups, ahead)
    position = ((ahead - 1) * bricks + sender_brk) * capacity + rank_of(arriving)
    value_v[...] = jnp.where(arriving, position, 0).astype(F32)
    slot_v[...] = jnp.where(arriving, jnp.bitwise_and(every, tiles - 1), -1)
    down_iota = lax.broadcasted_iota(jnp.int32, (tiles, tiles), 0)
    across_iota = lax.broadcasted_iota(jnp.int32, (tiles, tiles), 1)

    def find(s, found):
        slots = jnp.broadcast_to(slot_v[pl.ds(s, 1), :], (tiles, tiles))
        values = jnp.broadcast_to(value_v[pl.ds(s, 1), :], (tiles, tiles))
        return found + jnp.where(slots == down_iota, values, 0.0)

    found = lax.fori_loop(0, owners, find, jnp.zeros((tiles, tiles), F32))
    column = jnp.sum(found, axis=1, keepdims=True)
    line = jnp.sum(jnp.where(down_iota == across_iota, column, 0.0), axis=0, keepdims=True)
    line_v[...] = line.astype(jnp.int32)
    line_copy = pltpu.make_async_copy(line_v, line_s, line_sem)
    line_copy.start()
    line_copy.wait()

    for i, fs in enumerate(phases):

        def arrive(p, carry):
            pltpu.make_async_remote_copy(
                src_ref=outbox[i].at[p],
                dst_ref=recv[i].at[p],
                send_sem=send_sem.at[i, p],
                recv_sem=recv_sem.at[i, p],
                device_id=(lax.rem(grp + 1, groups), brk),
                device_id_type=MESH,
            ).wait_recv()
            return carry

        lax.fori_loop(0, partners, arrive, 0)
        block = len(fs) * tile_rows

        def place_tiles(n, carry):
            for u in range(8):
                slot = n * 8 + u
                at = jnp.clip(line_s[0, slot], 0, partners * capacity - 1)
                box, first = at // capacity, lax.rem(at, capacity) * block
                for j in range(block):
                    stage[j, pl.ds(slot, 1), :] = recv[i][box, first + j, :, :]
            return carry

        lax.fori_loop(0, tiles // 8, place_tiles, 0)
        for j, f in enumerate(fs):
            for k in range(tile_rows):
                out[f, :, k * lanes : (k + 1) * lanes] = stage[j * tile_rows + k]

    for i in range(stages):

        def sent(p, carry):
            outgoing(i, p)[1].wait_send()
            return carry

        lax.fori_loop(0, partners, sent, 0)


def local(groups, bricks, state, adjoint, source, kappa, cut_flags, coupling, target):
    _, fields, cells_x, cells_y, lanes = state.shape
    tiles = target.shape[1]
    owners = groups * bricks
    partners = (groups - 1) * bricks
    capacity = tiles // partners + 1
    planes = cells_x // 2
    rows = cells_y // 4
    length = planes * rows * lanes // tiles
    tile_rows = length // lanes
    chunks = cells_x // CHUNK
    phases = split_fields(fields)
    stages = len(phases)
    widest = max(len(fs) for fs in phases)
    hbm = pl.BlockSpec(memory_space=pl.ANY)
    vmem = pl.BlockSpec(memory_space=pltpu.VMEM)
    smem = pl.BlockSpec(memory_space=pltpu.SMEM)
    brick = (fields, cells_x, cells_y, lanes)
    cells = math.prod(brick)
    boxes = [
        pltpu.VMEM((partners, capacity * len(fs) * tile_rows, 1, lanes), F32) for fs in phases
    ]
    placed = pl.pallas_call(
        functools.partial(route_kernel, groups, bricks, capacity, phases),
        out_shape=jax.ShapeDtypeStruct((fields, tiles, length), F32),
        in_specs=[hbm, hbm, hbm, hbm, hbm, smem, vmem],
        out_specs=vmem,
        scratch_shapes=boxes + boxes + [
            pltpu.VMEM((fields, cells_x + 2, cells_y + 2 * PAD, lanes), F32),
            pltpu.VMEM(brick, F32),
            pltpu.VMEM(brick, F32),
            pltpu.VMEM(brick[1:], F32),
            pltpu.VMEM(brick[1:], jnp.int32),
            pltpu.VMEM((planes, widest * cells_y + 8, lanes), F32),
            pltpu.VMEM((fields, planes * rows, lanes), F32),
            pltpu.VMEM((owners, tiles), jnp.int32),
            pltpu.SMEM((owners, tiles), jnp.int32),
            pltpu.VMEM((owners, tiles), jnp.int32),
            pltpu.VMEM((owners, tiles), F32),
            pltpu.VMEM((1, tiles), jnp.int32),
            pltpu.SMEM((1, tiles), jnp.int32),
            pltpu.VMEM((widest * tile_rows, tiles, lanes), F32),
            pltpu.SemaphoreType.DMA((5, chunks)),
            pltpu.SemaphoreType.DMA((2, stages)),
            pltpu.SemaphoreType.DMA,
            pltpu.SemaphoreType.DMA,
            pltpu.SemaphoreType.DMA((2, stages)),
            pltpu.SemaphoreType.DMA((2, stages)),
            pltpu.SemaphoreType.DMA((stages, partners)),
            pltpu.SemaphoreType.DMA((stages, partners)),
        ],
        compiler_params=pltpu.CompilerParams(
            collective_id=0, has_side_effects=True, vmem_limit_bytes=56 * 1024 * 1024
        ),
        cost_estimate=pl.CostEstimate(flops=25 * cells, bytes_accessed=14 * cells, transcendentals=0),
    )(state, adjoint, source, kappa, cut_flags, coupling, target)
    return placed.transpose(1, 0, 2)


def solution(mesh):
    placed = (
        P("grp", None, "brk", None, None),
        P("grp", None, "brk", None, None),
        P("grp", None, "brk", None, None),
        P("grp", "brk", None, None),
        P("grp", "brk", None, None),
        P(),
        P(),
    )
    return jax.shard_map(
        functools.partial(local, mesh.shape["grp"], mesh.shape["brk"]),
        mesh=mesh, in_specs=placed, out_specs=P(("grp", "brk"), None, None), check_vma=False,
    )
```

```python
import functools
import math

import jax
import jax.numpy as jnp
from jax import lax
from jax.experimental import pallas as pl
from jax.experimental.pallas import tpu as pltpu
from jax.sharding import PartitionSpec as P

F32 = jnp.float32
MESH = pl.DeviceIdType.MESH
PAD = 8
CHUNK = 6


def split_fields(fields):
    first = list(range(0, 1))
    rest = list(range(1, fields))
    half = (len(rest) + 1) // 2
    return [part for part in (first, rest[:half], rest[half:]) if part]


def route_kernel(
    groups, bricks, capacity, phases,
    state, adjoint, source, kappa, flags, coupling, target,
    out, *scratch,
):
    stages = len(phases)
    outbox, recv = scratch[:stages], scratch[stages : 2 * stages]
    (
        st, ad, so, ka, fl, acc, packed, table_v, table_s, slot_v, value_v, line_v, line_s, stage,
        load_sem, late_sem, table_sem, line_sem, halo_send, halo_recv, send_sem, recv_sem,
    ) = scratch[2 * stages :]
    fields, cells_x, cells_y, lanes = so.shape
    tiles = target.shape[1]
    owners = groups * bricks
    partners = (groups - 1) * bricks
    planes = cells_x // 2
    chunks = cells_x // CHUNK
    per_chunk = CHUNK // 2
    rows = cells_y // 4
    tile_rows = planes * rows // tiles
    grp, brk = lax.axis_index("grp"), lax.axis_index("brk")
    me = grp * bricks + brk

    barrier = pltpu.get_barrier_semaphore()

    def greet(i, carry):
        other = lax.rem(me + i, owners)
        pl.semaphore_signal(
            barrier, inc=1, device_id=(other // bricks, lax.rem(other, bricks)), device_id_type=MESH
        )
        return carry

    def state_load(c):
        return pltpu.make_async_copy(
            state.at[0, :, pl.ds(c * CHUNK, CHUNK)],
            st.at[:, pl.ds(c * CHUNK + 1, CHUNK), pl.ds(PAD, cells_y)],
            load_sem.at[0, c],
        )

    def other_loads(c):
        span = pl.ds(c * CHUNK, CHUNK)
        here = pl.ds(phases[0][0], len(phases[0]))
        return (
            pltpu.make_async_copy(adjoint.at[0, here, span], ad.at[here, span], load_sem.at[1, c]),
            pltpu.make_async_copy(source.at[0, here, span], so.at[here, span], load_sem.at[2, c]),
            pltpu.make_async_copy(kappa.at[0, span], ka.at[span], load_sem.at[3, c]),
            pltpu.make_async_copy(flags.at[0, span], fl.at[span], load_sem.at[4, c]),
        )

    def late_loads(i):
        here = pl.ds(phases[i][0], len(phases[i]))
        return (
            pltpu.make_async_copy(adjoint.at[0, here], ad.at[here], late_sem.at[0, i]),
            pltpu.make_async_copy(source.at[0, here], so.at[here], late_sem.at[1, i]),
        )

    state_load(0).start()
    state_load(1).start()
    for c in list(range(1, chunks)) + [0]:
        if 1 <= c < chunks - 1:
            state_load(c + 1).start()
        for copy in other_loads(c):
            copy.start()
    for i in range(1, stages):
        for copy in late_loads(i):
            copy.start()
    lax.fori_loop(1, owners, greet, 0)

    zeros_pad = jnp.zeros((fields, cells_x + 2, PAD, lanes), F32)
    st[:, :, 0:PAD, :] = zeros_pad
    st[:, :, PAD + cells_y : 2 * PAD + cells_y, :] = zeros_pad
    zeros_face = jnp.zeros((fields, cells_y, lanes), F32)

    @pl.when(brk == 0)
    def _():
        st[:, 0, PAD : PAD + cells_y, :] = zeros_face

    @pl.when(brk == bricks - 1)
    def _():
        st[:, cells_x + 1, PAD : PAD + cells_y, :] = zeros_face

    shift = int(math.log2(tiles))
    earlier = (
        lax.broadcasted_iota(jnp.int32, (tiles, tiles), 0)
        < lax.broadcasted_iota(jnp.int32, (tiles, tiles), 1)
    ).astype(F32).astype(jnp.bfloat16)
    owner_row = lax.broadcasted_iota(jnp.int32, (owners, tiles), 0)
    tile_col = lax.broadcasted_iota(jnp.int32, (owners, tiles), 1)

    def rank_of(chosen):
        return jnp.dot(
            chosen.astype(F32).astype(jnp.bfloat16), earlier, preferred_element_type=F32
        ).astype(jnp.int32)

    mine = lax.shift_right_logical(target[pl.ds(me, 1), :], jnp.int32(shift))
    chosen = jnp.broadcast_to(mine, (owners, tiles)) == owner_row
    rank = rank_of(chosen)
    table = jnp.zeros((owners, tiles), F32)
    for r in range(capacity):
        hit = jnp.logical_and(chosen, rank == r)
        index = jnp.sum(jnp.where(hit, tile_col.astype(F32), 0.0), axis=1, keepdims=True)
        table = jnp.where(tile_col == r, index, table)
    table_v[...] = table.astype(jnp.int32)
    table_copy = pltpu.make_async_copy(table_v, table_s, table_sem)
    table_copy.start()

    coef = [
        [coupling[f, h] + (6.0 if f == h else 0.0) for h in range(fields)] for f in range(fields)
    ]
    lane = lax.broadcasted_iota(jnp.int32, (8, lanes), 1)
    not_first, not_last = lane > 0, lane < lanes - 1
    most = max(len(fs) for fs in phases) * rows
    spot = lax.broadcasted_iota(jnp.int32, (most, lanes), 1)
    even_lane = jnp.bitwise_and(spot, 1) == 0
    half = lanes // 2
    order = jnp.where(spot < half, 2 * spot, 2 * (spot - half) + 1)

    def restrict(plane, fs):
        count = len(fs) * rows
        quarter = [acc[plane, pl.ds(q, count, stride=4), :] for q in range(4)]
        first, second = quarter[0] + quarter[1], quarter[2] + quarter[3]
        first = first + pltpu.roll(first, lanes - 1, 1)
        second = second + pltpu.roll(second, 1, 1)
        mixed = jnp.where(even_lane[:count], first, second)
        result = jnp.take_along_axis(mixed, order[:count], axis=1, mode="promise_in_bounds")
        for i, f in enumerate(fs):
            packed[f, pl.ds(pl.multiple_of(plane * rows, rows), rows), :] = result[
                i * rows : (i + 1) * rows
            ]

    def restrict_all(fs):
        def body(n, carry):
            for u in range(4):
                restrict(n * 4 + u, fs)
            return carry

        lax.fori_loop(0, planes // 4, body, 0)

    def stencil(plane, fs):
        x = 2 * plane
        for y in range(0, cells_y, 8):
            inside = slice(PAD + y, PAD + y + 8)
            centre = [[st[f, x + 1 + d, inside, :] for d in range(2)] for f in range(fields)]
            totals = [None] * len(fs)
            for d in range(2):
                react = ka[x + d, y : y + 8, :]
                weight = 1.0 - 0.5 * fl[x + d, y : y + 8, :].astype(F32)
                for i, f in enumerate(fs):
                    own = centre[f][d]
                    near = centre[f][1 - d] + st[f, x + 3 * d, inside, :]
                    near = near + (
                        st[f, x + 1 + d, PAD + y - 1 : PAD + y + 7, :]
                        + st[f, x + 1 + d, PAD + y + 1 : PAD + y + 9, :]
                    )
                    near = near + (
                        jnp.where(not_first, pltpu.roll(own, 1, 1), 0.0)
                        + jnp.where(not_last, pltpu.roll(own, lanes - 1, 1), 0.0)
                    )
                    mixed = react * own
                    for h in range(fields):
                        mixed = mixed + coef[f][h] * centre[h][d]
                    residual = so[f, x + d, y : y + 8, :] - (mixed - near)
                    part = weight * ad[f, x + d, y : y + 8, :] * residual
                    totals[i] = part if d == 0 else totals[i] + part
            for i in range(len(fs)):
                acc[plane, i * cells_y + y : i * cells_y + y + 8, :] = totals[i]

    def steps(start, stop, fs, with_loads, with_state):
        def body(n, carry):
            c = lax.rem(n + 1, chunks)
            if with_loads:
                if with_state:
                    state_load(c + 1).wait()
                for copy in other_loads(c):
                    copy.wait()
            for u in range(per_chunk):
                stencil(c * per_chunk + u, fs)
            return carry

        lax.fori_loop(start, stop, body, 0)

    inner = pl.ds(PAD, cells_y)

    def faces(i):
        here = pl.ds(phases[i][0], len(phases[i]))
        up = pltpu.make_async_remote_copy(
            src_ref=state.at[0, here, cells_x - 1],
            dst_ref=st.at[here, 0, inner],
            send_sem=halo_send.at[0, i],
            recv_sem=halo_recv.at[0, i],
            device_id=(grp, brk + 1),
            device_id_type=MESH,
        )
        down = pltpu.make_async_remote_copy(
            src_ref=state.at[0, here, 0],
            dst_ref=st.at[here, cells_x + 1, inner],
            send_sem=halo_send.at[1, i],
            recv_sem=halo_recv.at[1, i],
            device_id=(grp, brk - 1),
            device_id_type=MESH,
        )
        return up, down

    def start_faces():
        for i in range(stages):
            up, down = faces(i)

            @pl.when(brk < bricks - 1)
            def _():
                up.start()

            @pl.when(brk > 0)
            def _():
                down.start()

    def wait_faces(i):
        up, down = faces(i)

        @pl.when(brk > 0)
        def _():
            up.wait_recv()
            down.wait_send()

        @pl.when(brk < bricks - 1)
        def _():
            down.wait_recv()
            up.wait_send()

    def outgoing(i, p):
        ahead = lax.rem(p + brk, groups - 1) + 1
        to_grp, to_brk = lax.rem(grp + ahead, groups), lax.rem(brk + p // (groups - 1), bricks)
        place = (ahead - 1) * bricks + brk
        return to_grp * bricks + to_brk, pltpu.make_async_remote_copy(
            src_ref=outbox[i].at[p],
            dst_ref=recv[i].at[place],
            send_sem=send_sem.at[i, p],
            recv_sem=recv_sem.at[i, place],
            device_id=(to_grp, to_brk),
            device_id_type=MESH,
        )

    def send_all(i, fs):
        def send(p, carry):
            owner, copy = outgoing(i, p)
            for r in range(capacity):
                t = jnp.clip(table_s[owner, r], 0, tiles - 1) * tile_rows
                for j, f in enumerate(fs):
                    for k in range(tile_rows):
                        outbox[i][p, (r * len(fs) + j) * tile_rows + k, :, :] = packed[
                            f, pl.ds(t + k, 1), :
                        ]
            copy.start()
            return carry

        lax.fori_loop(0, partners, send, 0)

    for i, fs in enumerate(phases):
        if i == 0:
            state_load(0).wait()
            state_load(1).wait()
            steps(0, 1, fs, True, True)
            pl.semaphore_wait(barrier, owners - 1)
            start_faces()
            steps(1, chunks - 2, fs, True, True)
            wait_faces(0)
            steps(chunks - 2, chunks, fs, True, False)
            table_copy.wait()
        else:
            for copy in late_loads(i):
                copy.wait()
            wait_faces(i)
            steps(0, chunks, fs, False, False)
        restrict_all(fs)
        send_all(i, fs)

    every = target[...]
    arriving = lax.shift_right_logical(every, jnp.int32(shift)) == me
    sender_grp = lax.shift_right_logical(owner_row, jnp.int32(int(math.log2(bricks))))
    sender_brk = jnp.bitwise_and(owner_row, bricks - 1)
    ahead = grp - sender_grp
    ahead = jnp.where(ahead < 0, ahead + groups, ahead)
    position = ((ahead - 1) * bricks + sender_brk) * capacity + rank_of(arriving)
    value_v[...] = jnp.where(arriving, position, 0).astype(F32)
    slot_v[...] = jnp.where(arriving, jnp.bitwise_and(every, tiles - 1), -1)
    down_iota = lax.broadcasted_iota(jnp.int32, (tiles, tiles), 0)
    across_iota = lax.broadcasted_iota(jnp.int32, (tiles, tiles), 1)

    def find(s, found):
        slots = jnp.broadcast_to(slot_v[pl.ds(s, 1), :], (tiles, tiles))
        values = jnp.broadcast_to(value_v[pl.ds(s, 1), :], (tiles, tiles))
        return found + jnp.where(slots == down_iota, values, 0.0)

    found = lax.fori_loop(0, owners, find, jnp.zeros((tiles, tiles), F32))
    column = jnp.sum(found, axis=1, keepdims=True)
    line = jnp.sum(jnp.where(down_iota == across_iota, column, 0.0), axis=0, keepdims=True)
    line_v[...] = line.astype(jnp.int32)
    line_copy = pltpu.make_async_copy(line_v, line_s, line_sem)
    line_copy.start()
    line_copy.wait()

    for i, fs in enumerate(phases):

        def arrive(p, carry):
            pltpu.make_async_remote_copy(
                src_ref=outbox[i].at[p],
                dst_ref=recv[i].at[p],
                send_sem=send_sem.at[i, p],
                recv_sem=recv_sem.at[i, p],
                device_id=(lax.rem(grp + 1, groups), brk),
                device_id_type=MESH,
            ).wait_recv()
            return carry

        lax.fori_loop(0, partners, arrive, 0)
        block = len(fs) * tile_rows

        def place_tiles(n, carry):
            for u in range(8):
                slot = n * 8 + u
                at = jnp.clip(line_s[0, slot], 0, partners * capacity - 1)
                box, first = at // capacity, lax.rem(at, capacity) * block
                for j in range(block):
                    stage[j, pl.ds(slot, 1), :] = recv[i][box, first + j, :, :]
            return carry

        lax.fori_loop(0, tiles // 8, place_tiles, 0)
        for j, f in enumerate(fs):
            for k in range(tile_rows):
                out[f, :, k * lanes : (k + 1) * lanes] = stage[j * tile_rows + k]

    for i in range(stages):

        def sent(p, carry):
            outgoing(i, p)[1].wait_send()
            return carry

        lax.fori_loop(0, partners, sent, 0)


def local(groups, bricks, state, adjoint, source, kappa, cut_flags, coupling, target):
    _, fields, cells_x, cells_y, lanes = state.shape
    tiles = target.shape[1]
    owners = groups * bricks
    partners = (groups - 1) * bricks
    capacity = tiles // partners + 1
    planes = cells_x // 2
    rows = cells_y // 4
    length = planes * rows * lanes // tiles
    tile_rows = length // lanes
    chunks = cells_x // CHUNK
    phases = split_fields(fields)
    stages = len(phases)
    widest = max(len(fs) for fs in phases)
    hbm = pl.BlockSpec(memory_space=pl.ANY)
    vmem = pl.BlockSpec(memory_space=pltpu.VMEM)
    smem = pl.BlockSpec(memory_space=pltpu.SMEM)
    brick = (fields, cells_x, cells_y, lanes)
    cells = math.prod(brick)
    boxes = [
        pltpu.VMEM((partners, capacity * len(fs) * tile_rows, 1, lanes), F32) for fs in phases
    ]
    placed = pl.pallas_call(
        functools.partial(route_kernel, groups, bricks, capacity, phases),
        out_shape=jax.ShapeDtypeStruct((fields, tiles, length), F32),
        in_specs=[hbm, hbm, hbm, hbm, hbm, smem, vmem],
        out_specs=vmem,
        scratch_shapes=boxes + boxes + [
            pltpu.VMEM((fields, cells_x + 2, cells_y + 2 * PAD, lanes), F32),
            pltpu.VMEM(brick, F32),
            pltpu.VMEM(brick, F32),
            pltpu.VMEM(brick[1:], F32),
            pltpu.VMEM(brick[1:], jnp.int32),
            pltpu.VMEM((planes, widest * cells_y + 8, lanes), F32),
            pltpu.VMEM((fields, planes * rows, lanes), F32),
            pltpu.VMEM((owners, tiles), jnp.int32),
            pltpu.SMEM((owners, tiles), jnp.int32),
            pltpu.VMEM((owners, tiles), jnp.int32),
            pltpu.VMEM((owners, tiles), F32),
            pltpu.VMEM((1, tiles), jnp.int32),
            pltpu.SMEM((1, tiles), jnp.int32),
            pltpu.VMEM((widest * tile_rows, tiles, lanes), F32),
            pltpu.SemaphoreType.DMA((5, chunks)),
            pltpu.SemaphoreType.DMA((2, stages)),
            pltpu.SemaphoreType.DMA,
            pltpu.SemaphoreType.DMA,
            pltpu.SemaphoreType.DMA((2, stages)),
            pltpu.SemaphoreType.DMA((2, stages)),
            pltpu.SemaphoreType.DMA((stages, partners)),
            pltpu.SemaphoreType.DMA((stages, partners)),
        ],
        compiler_params=pltpu.CompilerParams(
            collective_id=0, has_side_effects=True, vmem_limit_bytes=56 * 1024 * 1024
        ),
        cost_estimate=pl.CostEstimate(flops=25 * cells, bytes_accessed=14 * cells, transcendentals=0),
    )(state, adjoint, source, kappa, cut_flags, coupling, target)
    return placed.transpose(1, 0, 2)


def solution(mesh):
    placed = (
        P("grp", None, "brk", None, None),
        P("grp", None, "brk", None, None),
        P("grp", None, "brk", None, None),
        P("grp", "brk", None, None),
        P("grp", "brk", None, None),
        P(),
        P(),
    )
    return jax.shard_map(
        functools.partial(local, mesh.shape["grp"], mesh.shape["brk"]),
        mesh=mesh, in_specs=placed, out_specs=P(("grp", "brk"), None, None), check_vma=False,
    )
```
